32 devices in a mesh: term: 4 (over z), row: 4 (over y, x), col: 2 (over core).
Axes of the slice: x: 2, y: 2, z: 4, core: 2. Of those that a mesh axis runs over, the one named last changes fastest.
Arguments:
- panel_column: float32 [4, 49152, 128], P('term', 'row'), may hold values from -3 to 8, as said below
- trailing: float32 [4, 49152, 256], P('term', 'row', 'col'), may hold values from -6 to 6
- right_side: float32 [49152, 512], P('row', 'col'), may hold values from -6 to 6
- term_weights: float32 [4], P('term'), may hold values from 0.5 to 1.5
Outputs:
- factor_column: float32 [4, 49152, 128], P('term', 'row')
- updated: float32 [4, 49152, 256], P('term', 'row', 'col')
- combined: float32 [49152, 512], P('row', 'col')
The draws below stay inside these ranges and needn't reach their ends.
Inputs may be any that keep to these rules, and one draw needn't show every extreme that they name: For each term, rows 0 to 127 of panel_column form a symmetric positive definite block.
All inputs are finite; a program needn't handle non-finite values.
Results may differ from the reference program's by a relative error of at most 0.0001.
Values sent between devices are 32-bit elements; how exact they have to be, the bound alone decides.
No kernel may reach another device: no remote copies, remote signals or barrier semaphores. Data moves between devices by JAX's collectives and lax.ppermute only.
A program may use at most 128 MiB of HBM per device.

```python
import jax
import jax.numpy as jnp
from jax import lax

N = 49152
B = 128
WIN_DEV = 128
RHS_DEV = 256
TERMS = 4
WIN = 256
RHS = 512
N_TERM = 4
N_ROW = 4
N_COL = 2


def draw_panel_column(key, part):
    key_low = jax.random.fold_in(key, 11)
    key_square = jax.random.fold_in(key, 12)
    key_diag = jax.random.fold_in(key, 13)
    lower = 0.25 * jax.random.normal(key_low, (TERMS, N, B), jnp.float32)
    square = jax.random.normal(key_square, (TERMS, B, B), jnp.float32)
    gram = jnp.einsum('tij,tkj->tik', square, square) / B
    shifts = jax.random.uniform(key_diag, (TERMS, B), jnp.float32, 0.5, 2.0) + 0.5 * jnp.arange(TERMS, dtype=jnp.float32)[:, None]
    block = gram + shifts[:, :, None] * jnp.eye(B, dtype=jnp.float32)[None, :, :]
    return lower.at[:, :B, :].set(block)


def block_scale(rng, extent, shards, low, largest):
    gain = 1.0
    for position, parts in shards:
        steps = jax.random.uniform(jax.random.fold_in(jax.random.fold_in(rng, 6), position), (parts,), jnp.float32, low / len(shards), largest / len(shards))
        gain = gain * jnp.repeat(jnp.exp(steps), extent[position] // parts).reshape((-1,) + (1,) * (len(extent) - 1 - position))
    return gain


def gaussian(key, extent, scale, limit, pieces=(), kind=jnp.bfloat16):
    array = scale * jax.random.normal(key, extent, jnp.float32)
    if pieces:
        array = array * block_scale(key, extent, pieces, -0.22, 0.18)
    return jnp.clip(array, -limit, limit).astype(kind)


def setup_inputs(seed: int = 0) -> dict:
    key_of = jax.random.split(jax.random.key(seed), 5)
    panel_column = draw_panel_column(jax.random.fold_in(key_of[4], 71), 0)
    trailing = gaussian(key_of[1], (TERMS, N, WIN), 1.0, 6.0, ((0, 4), (1, 4), (2, 2)), jnp.float32)
    right_side = gaussian(key_of[2], (N, RHS), 1.0, 6.0, ((0, 4), (1, 2)), jnp.float32)
    term_weights = jnp.clip(0.5 + 1.0 * jax.random.uniform(key_of[3], (TERMS,), jnp.float32) ** block_scale(key_of[3], (TERMS,), ((0, 4),), -0.2, 0.2), 0.5, 1.5)
    return dict(panel_column=panel_column, trailing=trailing, right_side=right_side, term_weights=term_weights)


HIGH = lax.Precision.HIGHEST

def contract_rows(left, right):
    return lax.dot_general(left.astype(jnp.float32), right.astype(jnp.float32), (((1,), (1,)), ((), ())), precision=HIGH, preferred_element_type=jnp.float32)

def reference(panel_column, trailing, right_side, term_weights):
    rows_dev = N // N_ROW
    per_row = WIN_DEV * N_COL // N_ROW
    window = (jnp.arange(N_ROW, dtype=jnp.int32)[:, None] * rows_dev + B + jnp.arange(per_row, dtype=jnp.int32)[None, :]).reshape(-1)
    factors = []
    updates = []
    combined = jnp.zeros((N, RHS_DEV * N_COL), jnp.float32)
    for term_index in range(N_TERM):
        column = panel_column[term_index]
        lower_block = jnp.linalg.cholesky(column[:B])
        below = lax.linalg.triangular_solve(lower_block, column[B:], left_side=False, lower=True, transpose_a=True)
        factor = jnp.concatenate([lower_block, below], axis=0)
        picked = jnp.take(factor, window, axis=0)
        updates.append(trailing[term_index] - contract_rows(factor, picked))
        factors.append(factor)
        top_solved = lax.linalg.triangular_solve(lower_block, right_side[:B], left_side=True, lower=True)
        rest = right_side[B:] - jnp.dot(below.astype(jnp.float32), top_solved.astype(jnp.float32), precision=HIGH, preferred_element_type=jnp.float32)
        solved = jnp.concatenate([top_solved, rest], axis=0)
        combined = combined + term_weights[term_index] * solved
    return (jnp.stack(factors), jnp.stack(updates), combined)
```

```python
import functools
import math

import jax
import jax.numpy as jnp
from jax import lax
from jax.experimental import pallas as pl
from jax.experimental.pallas import tpu as pltpu
from jax.sharding import PartitionSpec as P

HIGH = lax.Precision.HIGHEST
F32 = jnp.float32
LANES = 128
PAD = 8
VMEM_LIMIT = 40 * 1024 * 1024


def dot(left, right):
    return jnp.dot(left, right, precision=HIGH, preferred_element_type=F32)


def chunk_sizes(part, width):
    unit = part // 12
    if part % 12 == 0 and unit >= width:
        return [unit, 4 * unit, 4 * unit, 2 * unit, unit]
    return [width] * (part // width)


def block_rows(*extents):
    return math.gcd(512, *extents)


def hops(mine, t, n):
    slots = []
    right = left = mine
    merged = False
    for h in range(1, n):
        to_right = [(j, j + 1) for j in range(h - 1, n - 1)]
        to_left = [(j, j - 1) for j in range(1, n - h + 1)]
        source = jnp.where(t >= h, n - h, h)
        valid = (t >= h) | (t < n - h)
        if merged:
            right = left = lax.ppermute(right, "term", to_right + to_left)
            slots.append((right, source, valid))
            continue
        right = lax.ppermute(right, "term", to_right)
        left = lax.ppermute(left, "term", to_left)
        if 2 * h > n - 1:
            right = left = jnp.where(t >= h, right, left)
            merged = True
            slots.append((right, source, valid))
        else:
            slots.append((right, jnp.int32(n - h), t >= h))
            slots.append((left, jnp.int32(h), t < n - h))
    return slots


def factor_kernel(width, flag, panel, trailing, inverse_t, picked_t, lower, factor, updated):
    solved = dot(panel[...], inverse_t[...])
    factor[...] = solved

    @pl.when((pl.program_id(0) == 0) & (flag[0] == 1))
    def _():
        factor[:width] = lower[...]

    updated[...] = trailing[...] - dot(factor[...], picked_t[...])


def factor_call(leading, panel, trailing, inverse_t, picked_t, lower):
    rows, width = panel.shape
    window = trailing.shape[1]
    block = block_rows(rows) * (2 if rows % 1024 == 0 else 1)
    whole = lambda a: pl.BlockSpec(a.shape, lambda i, f: (0, 0))
    tile = lambda n: pl.BlockSpec((block, n), lambda i, f: (i, 0))
    return pl.pallas_call(
        functools.partial(factor_kernel, width),
        grid_spec=pltpu.PrefetchScalarGridSpec(
            num_scalar_prefetch=1,
            grid=(rows // block,),
            in_specs=[tile(width), tile(window), whole(inverse_t), whole(picked_t), whole(lower)],
            out_specs=[tile(width), tile(window)],
        ),
        out_shape=[
            jax.ShapeDtypeStruct((rows, width), F32),
            jax.ShapeDtypeStruct((rows, window), F32),
        ],
        compiler_params=pltpu.CompilerParams(vmem_limit_bytes=VMEM_LIMIT),
        cost_estimate=pl.CostEstimate(
            flops=2 * rows * width * (width + window) * 6,
            bytes_accessed=8 * rows * (width + window),
            transcendentals=0,
        ),
        name="factor_update",
    )(leading, panel, trailing, inverse_t, picked_t, lower)


def early_kernel(n_bufs, sides, *refs):
    bufs, weights, outs = refs[:n_bufs], refs[n_bufs], refs[n_bufs + 1 :]
    stacked = jnp.concatenate([b[...] for b in bufs], axis=1)
    total = dot(stacked, weights[...])
    for k, out in enumerate(outs):
        out[...] = total[:, k * sides : (k + 1) * sides]


def early_call(size, bufs, weights, n_col):
    width = bufs[0].shape[1]
    sides = weights.shape[1] // n_col
    block = block_rows(size)
    return pl.pallas_call(
        functools.partial(early_kernel, len(bufs), sides),
        grid=(size // block,),
        in_specs=[pl.BlockSpec((block, width), lambda i: (i, 0))] * len(bufs)
        + [pl.BlockSpec(weights.shape, lambda i: (0, 0))],
        out_specs=[pl.BlockSpec((block, sides), lambda i: (i, 0))] * n_col,
        out_shape=[jax.ShapeDtypeStruct((size, sides), F32)] * n_col,
        compiler_params=pltpu.CompilerParams(vmem_limit_bytes=VMEM_LIMIT),
        cost_estimate=pl.CostEstimate(
            flops=2 * size * weights.shape[0] * weights.shape[1] * 6,
            bytes_accessed=4 * size * (width * len(bufs) + weights.shape[1]),
            transcendentals=0,
        ),
        name="early_terms",
    )(*bufs, weights)


def late_kernel(n_col, n_late, first, width, scalars, total_weight, rhs, top, weights, *refs):
    early, late = refs[:n_col], refs[n_col : n_col * (1 + n_late)]
    out = refs[-1]
    phase = pl.program_id(0)
    for k in range(n_col):

        @pl.when(phase == k)
        def _(k=k):
            out[...] = total_weight[0] * rhs[...] - early[k][...]
            for i in range(n_late):
                out[...] -= dot(
                    late[i * n_col + k][...], weights[i * width : (i + 1) * width]
                )

    if first:
        part = lax.rem(scalars[0] - phase + n_col, n_col)

        @pl.when((part == 0) & (scalars[1] == 1) & (pl.program_id(1) == 0))
        def _():
            out[:width] = top[...]


def late_call(scalars, total_weight, rhs, top, weights, early, late, start, size, part, combined):
    n_col, n_late = len(early), len(late)
    sides = rhs.shape[1]
    width = weights.shape[0] // n_late
    block = block_rows(size, start, part)
    steps = size // block
    at = lambda k, j, s: (
        (lax.rem(s[0] - k + n_col, n_col) * (part // block) + start // block + j),
        0,
    )

    def held(phase):
        return lambda k, j, s: (
            jnp.where(k == phase, j, jnp.where(k < phase, 0, steps - 1)),
            0,
        )

    rhs_spec = pl.BlockSpec((block, sides), at)
    in_specs = [
        pl.BlockSpec(memory_space=pltpu.SMEM),
        rhs_spec,
        pl.BlockSpec(top.shape, lambda k, j, s: (0, 0)),
        pl.BlockSpec(weights.shape, lambda k, j, s: (0, 0)),
    ]
    in_specs += [pl.BlockSpec((block, sides), held(k)) for k in range(n_col)]
    in_specs += [pl.BlockSpec((block, width), held(k)) for _ in late for k in range(n_col)]
    operands = [total_weight, rhs, top, weights, *early, *[b for bufs in late for b in bufs]]
    aliases = {}
    if combined is not None:
        in_specs.append(pl.BlockSpec(memory_space=pl.ANY))
        operands.append(combined)
        aliases = {len(operands): 0}
    return pl.pallas_call(
        functools.partial(late_kernel, n_col, n_late, start == 0, width),
        grid_spec=pltpu.PrefetchScalarGridSpec(
            num_scalar_prefetch=1,
            grid=(n_col, steps),
            in_specs=in_specs,
            out_specs=rhs_spec,
        ),
        out_shape=jax.ShapeDtypeStruct(rhs.shape, F32),
        input_output_aliases=aliases,
        compiler_params=pltpu.CompilerParams(vmem_limit_bytes=VMEM_LIMIT),
        cost_estimate=pl.CostEstimate(
            flops=2 * size * n_col * width * n_late * sides * 6,
            bytes_accessed=4 * size * n_col * (width * n_late + 3 * sides),
            transcendentals=0,
        ),
        name="late_terms",
    )(scalars, *operands)


def to_col(x, k):
    n = lax.axis_size("col")
    return x if k == 0 else lax.ppermute(x, "col", [(i, (i + k) % n) for i in range(n)])


def body(panel_column, trailing, right_side, term_weights):
    column = panel_column[0]
    rows, width = column.shape
    n_term, n_row, n_col = (lax.axis_size(a) for a in ("term", "row", "col"))
    t, r, c = (lax.axis_index(a) for a in ("term", "row", "col"))
    window = trailing.shape[2]
    per_row = window * n_col // n_row
    part = rows // n_col
    sizes = chunk_sizes(part, width)
    starts = [sum(sizes[:i]) for i in range(len(sizes))]
    scalars = jnp.stack([c, (r == 0).astype(jnp.int32)]).astype(jnp.int32)

    mine = [lax.dynamic_slice_in_dim(column, c * part + o, s, 0) for o, s in zip(starts, sizes)]
    mine[0] = jnp.concatenate([mine[0], jnp.full((PAD, width), term_weights[0], F32)], axis=0)
    slots = [hops(m, t, n_term) for m in mine]

    tops = right_side[:width]
    n_side = tops.shape[1] // LANES
    packed = [column[width : width + per_row]] + [
        tops[:, i * LANES : (i + 1) * LANES] for i in range(n_side)
    ]
    packed = lax.all_gather(jnp.concatenate(packed, axis=0), "row", axis=0)
    window_rows = packed[:, :per_row].reshape(n_row * per_row, width)
    window_rows = lax.dynamic_slice_in_dim(window_rows, c * window, window, 0)
    right_top = jnp.concatenate(
        [packed[0, per_row + i * width : per_row + (i + 1) * width] for i in range(n_side)], axis=1
    )
    right_tops = jnp.concatenate([to_col(right_top, n_col - k if k else 0) for k in range(n_col)], axis=1)

    heads = [mine[0]]
    for s in range(1, n_term):
        heads.append(
            sum(
                jnp.where((source == s) & valid, buf, 0.0)
                for buf, source, valid in slots[0]
            )
        )
    weights = jnp.stack([h[sizes[0], 0] for h in heads])
    total_weight = jnp.sum(weights)
    corners = jnp.concatenate([h[:width] for h in heads], axis=0)
    others = lax.ppermute(corners, "col", [(0, 1)]) if n_col == 2 else lax.all_gather(corners, "col")[0]
    corners = jnp.where(c == 0, corners, others)
    corner = corners[:width]
    for s in range(1, n_term):
        got = lax.ppermute(corners[s * width : (s + 1) * width], "row", [(0, s)])
        corner = jnp.where(r == s, got, corner)
    lower = jnp.linalg.cholesky(corner)
    inverse = lax.linalg.triangular_solve(
        lower, jnp.eye(width, dtype=F32), left_side=True, lower=True
    )
    inverses = lax.all_gather(inverse, "row", axis=0)[:n_term]

    inverse_t = inverses[0].T
    picked_t = dot(window_rows, inverse_t).T
    factor, updated = factor_call(scalars[1:], column, trailing[0], inverse_t, picked_t, lower)

    solved = [weights[s] * dot(inverses[s], right_tops) for s in range(n_term)]
    tall = jnp.stack([dot(inverses[s].T, solved[s]) for s in range(n_term)])
    top = sum(solved)[:, : tops.shape[1]]

    def of(source, valid):
        return jnp.where(valid, lax.dynamic_index_in_dim(tall, source, 0, keepdims=False), 0.0)

    n_late = 1 if n_term > 2 else 0
    n_slots = len(slots[0])
    early_ids, late_ids = range(n_slots - n_late), range(n_slots - n_late, n_slots)
    early_weights = jnp.concatenate([tall[0]] + [of(*slots[0][i][1:]) for i in early_ids], axis=0)
    late_weights = jnp.concatenate([of(*slots[0][i][1:]) for i in late_ids], axis=0)
    late_weights = late_weights[:, : tops.shape[1]]

    combined = None
    for i, (start, size) in enumerate(zip(starts, sizes)):
        products = early_call(
            size, [mine[i]] + [slots[i][j][0] for j in early_ids], early_weights, n_col
        )
        early = [to_col(products[k], k) for k in range(n_col)]
        late = [[to_col(slots[i][j][0], k) for k in range(n_col)] for j in late_ids]
        combined = late_call(
            scalars, total_weight[None], right_side, top, late_weights, early, late,
            start, size, part, combined,
        )
    return (factor[None], updated[None], combined)


def solution(mesh):
    placed = (P("term", "row", None), P("term", "row", "col"), P("row", "col"), P("term"))
    return jax.shard_map(
        body,
        mesh=mesh,
        in_specs=placed,
        out_specs=(P("term", "row", None), P("term", "row", "col"), P("row", "col")),
        check_vma=False,
    )
```

```python
import functools
import math

import jax
import jax.numpy as jnp
from jax import lax
from jax.experimental import pallas as pl
from jax.experimental.pallas import tpu as pltpu
from jax.sharding import PartitionSpec as P

HIGH = lax.Precision.HIGHEST
F32 = jnp.float32
BF16 = jnp.bfloat16
LANES = 128
PAD = 8
VMEM_LIMIT = 60 * 1024 * 1024
ANY = pl.BlockSpec(memory_space=pl.ANY)
COST = pl.CostEstimate(flops=1, bytes_accessed=1, transcendentals=0)


def dot(left, right):
    return jnp.dot(left, right, precision=HIGH, preferred_element_type=F32)


def chunk_sizes(part, width):
    unit = part // 12
    if part % 12 == 0 and unit % 8 == 0 and unit >= width:
        return [unit, 9 * unit, 2 * unit], [1, 3, 1]
    parts = part // width
    return [width, (parts - 2) * width, width], [1, 1, 1]


def block_rows(*extents):
    return math.gcd(512, *extents)


def send_hop(h, mine, t, n):
    to_right = [(j, j + 1) for j in range(h - 1, n - 1)]
    to_left = [(j, j - 1) for j in range(1, n - h + 1)]
    if 2 * (h - 1) > n - 1:
        return (lax.ppermute(mine[0], "term", to_right + to_left),)
    return (lax.ppermute(mine[0], "term", to_right), lax.ppermute(mine[-1], "term", to_left))


def merge_hop(h, got, t, n):
    if len(got) == 2 and 2 * h > n - 1:
        return (jnp.where(t >= h, got[0], got[1]),)
    return got


def slot_terms(t, n):
    slots = []
    for h in range(1, n):
        if 2 * h > n - 1:
            slots.append((h, 0, jnp.where(t >= h, n - h, h), (t >= h) | (t < n - h)))
        else:
            slots.append((h, 0, jnp.int32(n - h), t >= h))
            slots.append((h, 1, jnp.int32(h), t < n - h))
    return slots


def gate(token, after, passed):
    def kernel(*refs):
        pass

    first = 1 + len(after)
    outs = [token, *passed]
    got = pl.pallas_call(
        kernel,
        in_specs=[ANY] * (first + len(passed)),
        out_specs=[ANY] * len(outs),
        out_shape=[jax.ShapeDtypeStruct(a.shape, a.dtype) for a in outs],
        input_output_aliases={0: 0} | {first + i: 1 + i for i in range(len(passed))},
        compiler_params=pltpu.CompilerParams(vmem_limit_bytes=VMEM_LIMIT),
        cost_estimate=COST,
        name="gate",
    )(token, *after, *passed)
    return got[0], got[1:]


def factor_kernel(width, flag, panel, trailing, inverse_t, picked_t, lower, factor, updated):
    solved = dot(panel[...], inverse_t[...])
    factor[...] = solved

    @pl.when((pl.program_id(0) == 0) & (flag[0] == 1))
    def _():
        factor[:width] = lower[...]

    updated[...] = trailing[...] - dot(factor[...], picked_t[...])


def factor_call(leading, panel, trailing, inverse_t, picked_t, lower):
    rows, width = panel.shape
    window = trailing.shape[1]
    block = block_rows(rows) * (2 if rows % 1024 == 0 else 1)
    whole = lambda a: pl.BlockSpec(a.shape, lambda i, f: (0, 0))
    tile = lambda n: pl.BlockSpec((block, n), lambda i, f: (i, 0))
    return pl.pallas_call(
        functools.partial(factor_kernel, width),
        grid_spec=pltpu.PrefetchScalarGridSpec(
            num_scalar_prefetch=1,
            grid=(rows // block,),
            in_specs=[tile(width), tile(window), whole(inverse_t), whole(picked_t), whole(lower)],
            out_specs=[tile(width), tile(window)],
        ),
        out_shape=[
            jax.ShapeDtypeStruct((rows, width), F32),
            jax.ShapeDtypeStruct((rows, window), F32),
        ],
        compiler_params=pltpu.CompilerParams(vmem_limit_bytes=VMEM_LIMIT),
        cost_estimate=COST,
        name="factor_update",
    )(leading, panel, trailing, inverse_t, picked_t, lower)


def split(x):
    high = x.astype(BF16)
    return high, (x - high.astype(F32)).astype(BF16)


def subtract(scalars, total_weight, rhs, product, top, out, first, part, step):
    out[...] = total_weight[0] * rhs[...] - product
    if first:

        @pl.when((part == 0) & (scalars[1] == 1) & (step == 0))
        def _():
            out[: top.shape[0]] = top[...]


def product_kernel(n_terms, n_col, first, scalars, total_weight, rhs, top, weights, *refs):
    bufs, outs = refs[:n_terms], refs[-n_col:]
    sides = rhs.shape[1]
    high, low = split(jnp.concatenate([b[...] for b in bufs], axis=1))
    stacked = jnp.concatenate([high, low, high], axis=1)

    def product(k):
        return jnp.dot(
            stacked, weights[:, k * sides : (k + 1) * sides], preferred_element_type=F32
        )

    for k in range(1, n_col):
        outs[k][...] = product(k)
    step = pl.program_id(0)
    subtract(scalars, total_weight, rhs, product(0), top, outs[0], first, scalars[0], step)


def product_call(common, bufs, firsts, weights, start, size, part, n_col, combined, after):
    scalars, total_weight, rhs, top = common
    width = bufs[0].shape[1]
    sides = rhs.shape[1]
    block = block_rows(size, start, part, *firsts)
    at = lambda i, s: (s[0] * (part // block) + start // block + i, 0)
    in_specs = [
        pl.BlockSpec(memory_space=pltpu.SMEM),
        pl.BlockSpec((block, sides), at),
        pl.BlockSpec(top.shape, lambda i, s: (0, 0)),
        pl.BlockSpec(weights.shape, lambda i, s: (0, 0)),
    ]
    in_specs += [
        pl.BlockSpec((block, width), lambda i, s, f=f: (f // block + i, 0)) for f in firsts
    ]
    operands = [total_weight, rhs, top, weights, *bufs, *after]
    in_specs += [ANY] * len(after)
    aliases = {}
    if combined is not None:
        in_specs.append(ANY)
        operands.append(combined)
        aliases = {len(operands): 0}
    got = pl.pallas_call(
        functools.partial(product_kernel, len(bufs), n_col, start == 0),
        grid_spec=pltpu.PrefetchScalarGridSpec(
            num_scalar_prefetch=1,
            grid=(size // block,),
            in_specs=in_specs,
            out_specs=[pl.BlockSpec((block, sides), at)]
            + [pl.BlockSpec((block, sides), lambda i, s: (i, 0))] * (n_col - 1),
        ),
        out_shape=[jax.ShapeDtypeStruct(rhs.shape, F32)]
        + [jax.ShapeDtypeStruct((size, sides), F32)] * (n_col - 1),
        input_output_aliases=aliases,
        compiler_params=pltpu.CompilerParams(vmem_limit_bytes=VMEM_LIMIT),
        cost_estimate=COST,
        name="products",
    )(scalars, *operands)
    return got[0], [to_col(q, k + 1) for k, q in enumerate(got[1:])]


def finish_kernel(n_other, first, scalars, total_weight, rhs, top, *refs):
    products, out = refs[:n_other], refs[-1]
    phase = pl.program_id(0)
    n_col = n_other + 1
    part = lax.rem(scalars[0] - phase - 1 + n_col, n_col)
    for k in range(n_other):

        @pl.when(phase == k)
        def _(k=k):
            subtract(
                scalars, total_weight, rhs, products[k][...], top, out, first, part, pl.program_id(1)
            )


def finish_call(common, products, start, size, part, combined):
    scalars, total_weight, rhs, top = common
    n_other = len(products)
    n_col = n_other + 1
    sides = rhs.shape[1]
    block = block_rows(size, start, part)
    steps = size // block
    at = lambda k, j, s: (
        (lax.rem(s[0] - k - 1 + n_col, n_col) * (part // block) + start // block + j),
        0,
    )

    def held(phase):
        return lambda k, j, s: (
            jnp.where(k == phase, j, jnp.where(k < phase, 0, steps - 1)),
            0,
        )

    rhs_spec = pl.BlockSpec((block, sides), at)
    in_specs = [
        pl.BlockSpec(memory_space=pltpu.SMEM),
        rhs_spec,
        pl.BlockSpec(top.shape, lambda k, j, s: (0, 0)),
    ]
    in_specs += [pl.BlockSpec((block, sides), held(k)) for k in range(n_other)] + [ANY]
    operands = [total_weight, rhs, top, *products, combined]
    return pl.pallas_call(
        functools.partial(finish_kernel, n_other, start == 0),
        grid_spec=pltpu.PrefetchScalarGridSpec(
            num_scalar_prefetch=1,
            grid=(n_other, steps),
            in_specs=in_specs,
            out_specs=rhs_spec,
        ),
        out_shape=jax.ShapeDtypeStruct(rhs.shape, F32),
        input_output_aliases={len(operands): 0},
        compiler_params=pltpu.CompilerParams(vmem_limit_bytes=VMEM_LIMIT),
        cost_estimate=COST,
        name="finish",
    )(scalars, *operands)


def to_col(x, k):
    n = lax.axis_size("col")
    return x if k == 0 else lax.ppermute(x, "col", [(i, (i + k) % n) for i in range(n)])


def body(panel_column, trailing, right_side, term_weights):
    column = panel_column[0]
    rows, width = column.shape
    n_term, n_row, n_col = (lax.axis_size(a) for a in ("term", "row", "col"))
    t, r, c = (lax.axis_index(a) for a in ("term", "row", "col"))
    window = trailing.shape[2]
    sides = right_side.shape[1]
    per_row = window * n_col // n_row
    part = rows // n_col
    sizes, pieces = chunk_sizes(part, width)
    starts = [sum(sizes[:i]) for i in range(len(sizes))]
    scalars = jnp.stack([c, (r == 0).astype(jnp.int32)]).astype(jnp.int32)
    slots = slot_terms(t, n_term)

    mine = [lax.dynamic_slice_in_dim(column, c * part + o, s, 0) for o, s in zip(starts, sizes)]
    sent = (jnp.concatenate([mine[0], jnp.full((PAD, width), term_weights[0], F32)], axis=0),)
    arrived = [sent]
    for h in range(1, n_term):
        sent = merge_hop(h, send_hop(h, sent, t, n_term), t, n_term)
        arrived.append(sent)
    _, bulk = gate(jnp.zeros((8, LANES), F32), [], mine[1:])
    gathered = [lax.all_gather(m, "term", axis=0, tiled=True) for m in bulk]

    tops = right_side[:width]
    n_side = sides // LANES
    packed = [column[width : width + per_row]] + [
        tops[:, i * LANES : (i + 1) * LANES] for i in range(n_side)
    ]
    packed = lax.all_gather(jnp.concatenate(packed, axis=0), "row", axis=0)
    window_rows = packed[:, :per_row].reshape(n_row * per_row, width)
    window_rows = lax.dynamic_slice_in_dim(window_rows, c * window, window, 0)
    right_top = jnp.concatenate(
        [packed[0, per_row + i * width : per_row + (i + 1) * width] for i in range(n_side)], axis=1
    )
    right_tops = jnp.concatenate(
        [to_col(right_top, n_col - k if k else 0) for k in range(n_col)], axis=1
    )

    heads = [arrived[0][0]]
    for s in range(1, n_term):
        heads.append(
            sum(
                jnp.where((source == s) & valid, arrived[h][place], 0.0)
                for h, place, source, valid in slots
            )
        )
    weights = jnp.stack([h[sizes[0], 0] for h in heads])
    total_weight = jnp.sum(weights)[None]
    corners = jnp.concatenate([h[:width] for h in heads], axis=0)
    others = lax.ppermute(corners, "col", [(0, 1)]) if n_col == 2 else lax.all_gather(corners, "col")[0]
    corners = jnp.where(c == 0, corners, others)
    corner = corners[:width]
    for s in range(1, n_term):
        got = lax.ppermute(corners[s * width : (s + 1) * width], "row", [(0, s)])
        corner = jnp.where(r == s, got, corner)
    lower = jnp.linalg.cholesky(corner)
    inverse = lax.linalg.triangular_solve(
        lower, jnp.eye(width, dtype=F32), left_side=True, lower=True
    )
    inverses = lax.all_gather(inverse, "row", axis=0)[:n_term]

    inverse_t = inverses[0].T
    picked_t = dot(window_rows, inverse_t).T
    factor, updated = factor_call(scalars[1:], column, trailing[0], inverse_t, picked_t, lower)

    solved = [weights[s] * dot(inverses[s], right_tops) for s in range(n_term)]
    top = sum(solved)[:, :sides]
    tall = jnp.concatenate([dot(inverses[s].T, solved[s]) for s in range(n_term)], axis=0)

    def stack(x):
        high = lax.reduce_precision(x, 8, 7)
        high, low = high.astype(BF16), (x - high).astype(BF16)
        return jnp.concatenate([high, high, low], axis=0)

    near = stack(tall)
    by_term = stack(
        lax.dynamic_slice_in_dim(
            jnp.concatenate([tall, tall], axis=0), (n_term - t) * width, n_term * width, 0
        )
    )

    common = (scalars, total_weight, right_side, top)
    combined = None
    for i, (start, size) in enumerate(zip(starts, sizes)):
        step = size // pieces[i]
        waiting = []
        for o in range(0, size, step):
            if i == 0:
                bufs, firsts, tall = heads, [0] * n_term, near
            else:
                bufs, tall = [gathered[i - 1]] * n_term, by_term
                firsts = [size * s + o for s in range(n_term)]
            after = [factor] if i and o == 0 else []
            combined, products = product_call(
                common, bufs, firsts, tall, start + o, step, part, n_col, combined, after
            )
            waiting.append((products, start + o))
            if len(waiting) == 2:
                combined = finish_call(common, *waiting.pop(0), step, part, combined)
        for products, begin in waiting:
            combined = finish_call(common, products, begin, step, part, combined)
    return (factor[None], updated[None], combined)


def solution(mesh):
    placed = (P("term", "row", None), P("term", "row", "col"), P("row", "col"), P("term"))
    return jax.shard_map(
        body,
        mesh=mesh,
        in_specs=placed,
        out_specs=(P("term", "row", None), P("term", "row", "col"), P("row", "col")),
        check_vma=False,
    )
```

```python
import functools
import math

import jax
import jax.numpy as jnp
from jax import lax
from jax.experimental import pallas as pl
from jax.experimental.pallas import tpu as pltpu
from jax.sharding import PartitionSpec as P

HIGH = lax.Precision.HIGHEST
F32 = jnp.float32
BF16 = jnp.bfloat16
LANES = 128
PAD = 8
VMEM_LIMIT = 60 * 1024 * 1024
ANY = pl.BlockSpec(memory_space=pl.ANY)
COST = pl.CostEstimate(flops=1, bytes_accessed=1, transcendentals=0)


def dot(left, right):
    return jnp.dot(left, right, precision=HIGH, preferred_element_type=F32)


def chunk_sizes(part, width):
    unit = part // 12
    if part % 12 == 0 and unit % width == 0:
        return [11 * unit, unit]
    return [part - width, width]


def block_rows(*extents):
    return math.gcd(512, *extents)


def send_hop(h, mine, t, n):
    to_right = [(j, j + 1) for j in range(h - 1, n - 1)]
    to_left = [(j, j - 1) for j in range(1, n - h + 1)]
    if 2 * (h - 1) > n - 1:
        return (lax.ppermute(mine[0], "term", to_right + to_left),)
    return (lax.ppermute(mine[0], "term", to_right), lax.ppermute(mine[-1], "term", to_left))


def merge_hop(h, got, t, n):
    if len(got) == 2 and 2 * h > n - 1:
        return (jnp.where(t >= h, got[0], got[1]),)
    return got


def slot_terms(t, n):
    slots = []
    for h in range(1, n):
        if 2 * h > n - 1:
            slots.append((h, 0, jnp.where(t >= h, n - h, h), (t >= h) | (t < n - h)))
        else:
            slots.append((h, 0, jnp.int32(n - h), t >= h))
            slots.append((h, 1, jnp.int32(h), t < n - h))
    return slots


def gate(token, after, passed):
    def kernel(*refs):
        pass

    first = 1 + len(after)
    outs = [token, *passed]
    got = pl.pallas_call(
        kernel,
        in_specs=[ANY] * (first + len(passed)),
        out_specs=[ANY] * len(outs),
        out_shape=[jax.ShapeDtypeStruct(a.shape, a.dtype) for a in outs],
        input_output_aliases={0: 0} | {first + i: 1 + i for i in range(len(passed))},
        compiler_params=pltpu.CompilerParams(vmem_limit_bytes=VMEM_LIMIT),
        cost_estimate=COST,
        name="gate",
    )(token, *after, *passed)
    return got[0], got[1:]


def factor_kernel(width, flag, panel, trailing, inverse_t, picked_t, lower, factor, updated):
    solved = dot(panel[...], inverse_t[...])
    factor[...] = solved

    @pl.when((pl.program_id(0) == 0) & (flag[0] == 1))
    def _():
        factor[:width] = lower[...]

    updated[...] = trailing[...] - dot(factor[...], picked_t[...])


def factor_call(leading, panel, trailing, inverse_t, picked_t, lower):
    rows, width = panel.shape
    window = trailing.shape[1]
    block = block_rows(rows) * (2 if rows % 1024 == 0 else 1)
    whole = lambda a: pl.BlockSpec(a.shape, lambda i, f: (0, 0))
    tile = lambda n: pl.BlockSpec((block, n), lambda i, f: (i, 0))
    return pl.pallas_call(
        functools.partial(factor_kernel, width),
        grid_spec=pltpu.PrefetchScalarGridSpec(
            num_scalar_prefetch=1,
            grid=(rows // block,),
            in_specs=[tile(width), tile(window), whole(inverse_t), whole(picked_t), whole(lower)],
            out_specs=[tile(width), tile(window)],
        ),
        out_shape=[
            jax.ShapeDtypeStruct((rows, width), F32),
            jax.ShapeDtypeStruct((rows, window), F32),
        ],
        compiler_params=pltpu.CompilerParams(vmem_limit_bytes=VMEM_LIMIT),
        cost_estimate=COST,
        name="factor_update",
    )(leading, panel, trailing, inverse_t, picked_t, lower)


def split(x):
    high = x.astype(BF16)
    return high, (x - high.astype(F32)).astype(BF16)


def terms_kernel(n_terms, first, leading, total_weight, rhs, top, weights, *refs):
    bufs, out = refs[:n_terms], refs[-1]
    high, low = split(jnp.concatenate([b[...] for b in bufs], axis=1))
    stacked = jnp.concatenate([high, low, high], axis=1)
    product = jnp.dot(stacked, weights[...], preferred_element_type=F32)
    out[...] = total_weight[0] * rhs[...] - product
    if first:

        @pl.when((leading[0] == 1) & (pl.program_id(0) == 0) & (pl.program_id(1) == 0))
        def _():
            out[: top.shape[0]] = top[...]


def terms_call(common, gathered, weights, start, size, n_col, part, combined, after):
    leading, total_weight, rhs, top = common
    width, sides = gathered.shape[1], rhs.shape[1]
    n_terms = gathered.shape[0] // (n_col * size)
    block = block_rows(size, start, part)
    steps = size // block
    at = lambda k, j, s: (k * (part // block) + start // block + j, 0)
    in_specs = [
        pl.BlockSpec(memory_space=pltpu.SMEM),
        pl.BlockSpec((block, sides), at),
        pl.BlockSpec(top.shape, lambda k, j, s: (0, 0)),
        pl.BlockSpec(weights.shape, lambda k, j, s: (0, 0)),
    ]
    in_specs += [
        pl.BlockSpec((block, width), lambda k, j, s, i=i: ((i * n_col + k) * steps + j, 0))
        for i in range(n_terms)
    ]
    operands = [total_weight, rhs, top, weights, *[gathered] * n_terms, *after]
    in_specs += [ANY] * len(after)
    aliases = {}
    if combined is not None:
        in_specs.append(ANY)
        operands.append(combined)
        aliases = {len(operands): 0}
    return pl.pallas_call(
        functools.partial(terms_kernel, n_terms, start == 0),
        grid_spec=pltpu.PrefetchScalarGridSpec(
            num_scalar_prefetch=1,
            grid=(n_col, steps),
            in_specs=in_specs,
            out_specs=pl.BlockSpec((block, sides), at),
        ),
        out_shape=jax.ShapeDtypeStruct(rhs.shape, F32),
        input_output_aliases=aliases,
        compiler_params=pltpu.CompilerParams(vmem_limit_bytes=VMEM_LIMIT),
        cost_estimate=COST,
        name="terms",
    )(leading, *operands)


def body(panel_column, trailing, right_side, term_weights):
    column = panel_column[0]
    rows, width = column.shape
    n_term, n_row, n_col = (lax.axis_size(a) for a in ("term", "row", "col"))
    t, r, c = (lax.axis_index(a) for a in ("term", "row", "col"))
    window = trailing.shape[2]
    sides = right_side.shape[1]
    per_row = window * n_col // n_row
    part = rows // n_col
    sizes = chunk_sizes(part, width)
    starts = [sum(sizes[:i]) for i in range(len(sizes))]
    leading = (r == 0).astype(jnp.int32)[None]
    slots = slot_terms(t, n_term)

    mine = [lax.dynamic_slice_in_dim(column, c * part + o, s, 0) for o, s in zip(starts, sizes)]
    _, mine = gate(jnp.zeros((8, LANES), F32), [], mine)
    gathered = [lax.all_gather(m, ("term", "col"), axis=0, tiled=True) for m in mine]

    sent = jnp.concatenate([column[:width], jnp.full((PAD, width), term_weights[0], F32)], axis=0)
    arrived = [(sent,)]
    for h in range(1, n_term):
        arrived.append(merge_hop(h, send_hop(h, arrived[-1], t, n_term), t, n_term))

    tops = right_side[:width]
    n_side = sides // LANES
    packed = [column[width : width + per_row]] + [
        tops[:, i * LANES : (i + 1) * LANES] for i in range(n_side)
    ]
    packed = lax.all_gather(jnp.concatenate(packed, axis=0), "row", axis=0)
    window_rows = packed[:, :per_row].reshape(n_row * per_row, width)
    window_rows = lax.dynamic_slice_in_dim(window_rows, c * window, window, 0)
    right_top = jnp.concatenate(
        [packed[0, per_row + i * width : per_row + (i + 1) * width] for i in range(n_side)], axis=1
    )

    heads = [sent]
    for s in range(1, n_term):
        heads.append(
            sum(
                jnp.where((source == s) & valid, arrived[h][place], 0.0)
                for h, place, source, valid in slots
            )
        )
    weights = jnp.stack([h[width, 0] for h in heads])
    total_weight = jnp.sum(weights)[None]
    corner = heads[0][:width]
    for s in range(1, n_term):
        got = lax.ppermute(heads[s][:width], "row", [(0, s)])
        corner = jnp.where(r == s, got, corner)
    lower = jnp.linalg.cholesky(corner)
    inverse = lax.linalg.triangular_solve(
        lower, jnp.eye(width, dtype=F32), left_side=True, lower=True
    )
    inverses = lax.all_gather(inverse, "row", axis=0)[:n_term]

    inverse_t = inverses[0].T
    picked_t = dot(window_rows, inverse_t).T
    factor, updated = factor_call(leading, column, trailing[0], inverse_t, picked_t, lower)

    solved = [weights[s] * dot(inverses[s], right_top) for s in range(n_term)]
    top = sum(solved)
    tall = jnp.concatenate([dot(inverses[s].T, solved[s]) for s in range(n_term)], axis=0)
    tall = lax.dynamic_slice_in_dim(
        jnp.concatenate([tall, tall], axis=0), (n_term - t) * width, n_term * width, 0
    )
    high = lax.reduce_precision(tall, 8, 7)
    high, low = high.astype(BF16), (tall - high).astype(BF16)
    stacked = jnp.concatenate([high, high, low], axis=0)

    common = (leading, total_weight, right_side, top)
    combined = None
    for i, (start, size) in enumerate(zip(starts, sizes)):
        combined = terms_call(
            common, gathered[i], stacked, start, size, n_col, part, combined, [] if i else [factor]
        )
    return (factor[None], updated[None], combined)


def solution(mesh):
    placed = (P("term", "row", None), P("term", "row", "col"), P("row", "col"), P("term"))
    return jax.shard_map(
        body,
        mesh=mesh,
        in_specs=placed,
        out_specs=(P("term", "row", None), P("term", "row", "col"), P("row", "col")),
        check_vma=False,
    )
```

```python
import functools
import math

import jax
import jax.numpy as jnp
from jax import lax
from jax.experimental import pallas as pl
from jax.experimental.pallas import tpu as pltpu
from jax.sharding import PartitionSpec as P

HIGH = lax.Precision.HIGHEST
F32 = jnp.float32
BF16 = jnp.bfloat16
LANES = 128
PAD = 8
VMEM_LIMIT = 60 * 1024 * 1024
ANY = pl.BlockSpec(memory_space=pl.ANY)
COST = pl.CostEstimate(flops=1, bytes_accessed=1, transcendentals=0)


def dot(left, right):
    return jnp.dot(left, right, precision=HIGH, preferred_element_type=F32)


def chunk_sizes(part, width):
    unit = part // 12
    if part % 12 == 0 and unit % width == 0:
        return [8 * unit, unit, 3 * unit]
    return [part - 2 * width, width, width]


def block_rows(*extents):
    return math.gcd(512, *extents)


def send_hop(h, mine, t, n):
    to_right = [(j, j + 1) for j in range(h - 1, n - 1)]
    to_left = [(j, j - 1) for j in range(1, n - h + 1)]
    if 2 * (h - 1) > n - 1:
        return (lax.ppermute(mine[0], "term", to_right + to_left),)
    return (lax.ppermute(mine[0], "term", to_right), lax.ppermute(mine[-1], "term", to_left))


def merge_hop(h, got, t, n):
    if len(got) == 2 and 2 * h > n - 1:
        return (jnp.where(t >= h, got[0], got[1]),)
    return got


def slot_terms(t, n):
    slots = []
    for h in range(1, n):
        if 2 * h > n - 1:
            slots.append((h, 0, jnp.where(t >= h, n - h, h), (t >= h) | (t < n - h)))
        else:
            slots.append((h, 0, jnp.int32(n - h), t >= h))
            slots.append((h, 1, jnp.int32(h), t < n - h))
    return slots


def gate(token, after, passed):
    def kernel(*refs):
        pass

    first = 1 + len(after)
    outs = [token, *passed]
    got = pl.pallas_call(
        kernel,
        in_specs=[ANY] * (first + len(passed)),
        out_specs=[ANY] * len(outs),
        out_shape=[jax.ShapeDtypeStruct(a.shape, a.dtype) for a in outs],
        input_output_aliases={0: 0} | {first + i: 1 + i for i in range(len(passed))},
        compiler_params=pltpu.CompilerParams(vmem_limit_bytes=VMEM_LIMIT),
        cost_estimate=COST,
        name="gate",
    )(token, *after, *passed)
    return got[0], got[1:]


def factor_kernel(width, flag, panel, trailing, inverse_t, picked_t, lower, factor, updated):
    solved = dot(panel[...], inverse_t[...])
    factor[...] = solved

    @pl.when((pl.program_id(0) == 0) & (flag[0] == 1))
    def _():
        factor[:width] = lower[...]

    updated[...] = trailing[...] - dot(factor[...], picked_t[...])


def factor_call(leading, panel, trailing, inverse_t, picked_t, lower):
    rows, width = panel.shape
    window = trailing.shape[1]
    block = block_rows(rows) * (2 if rows % 1024 == 0 else 1)
    whole = lambda a: pl.BlockSpec(a.shape, lambda i, f: (0, 0))
    tile = lambda n: pl.BlockSpec((block, n), lambda i, f: (i, 0))
    return pl.pallas_call(
        functools.partial(factor_kernel, width),
        grid_spec=pltpu.PrefetchScalarGridSpec(
            num_scalar_prefetch=1,
            grid=(rows // block,),
            in_specs=[tile(width), tile(window), whole(inverse_t), whole(picked_t), whole(lower)],
            out_specs=[tile(width), tile(window)],
        ),
        out_shape=[
            jax.ShapeDtypeStruct((rows, width), F32),
            jax.ShapeDtypeStruct((rows, window), F32),
        ],
        compiler_params=pltpu.CompilerParams(vmem_limit_bytes=VMEM_LIMIT),
        cost_estimate=COST,
        name="factor_update",
    )(leading, panel, trailing, inverse_t, picked_t, lower)


def split(x):
    high = x.astype(BF16)
    return high, (x - high.astype(F32)).astype(BF16)


def terms_kernel(n_terms, first, leading, total_weight, rhs, top, weights, *refs):
    bufs, out = refs[:n_terms], refs[-1]
    high, low = split(jnp.concatenate([b[...] for b in bufs], axis=1))
    stacked = jnp.concatenate([high, low, high], axis=1)
    product = jnp.dot(stacked, weights[...], preferred_element_type=F32)
    out[...] = total_weight[0] * rhs[...] - product
    if first:

        @pl.when((leading[0] == 1) & (pl.program_id(0) == 0) & (pl.program_id(1) == 0))
        def _():
            out[: top.shape[0]] = top[...]


def terms_call(common, gathered, weights, start, size, n_col, part, combined, after):
    leading, total_weight, rhs, top = common
    width, sides = gathered.shape[1], rhs.shape[1]
    n_terms = gathered.shape[0] // (n_col * size)
    block = block_rows(size, start, part)
    steps = size // block
    at = lambda k, j, s: (k * (part // block) + start // block + j, 0)
    in_specs = [
        pl.BlockSpec(memory_space=pltpu.SMEM),
        pl.BlockSpec((block, sides), at),
        pl.BlockSpec(top.shape, lambda k, j, s: (0, 0)),
        pl.BlockSpec(weights.shape, lambda k, j, s: (0, 0)),
    ]
    in_specs += [
        pl.BlockSpec((block, width), lambda k, j, s, i=i: ((i * n_col + k) * steps + j, 0))
        for i in range(n_terms)
    ]
    operands = [total_weight, rhs, top, weights, *[gathered] * n_terms, *after]
    in_specs += [ANY] * len(after)
    aliases = {}
    if combined is not None:
        in_specs.append(ANY)
        operands.append(combined)
        aliases = {len(operands): 0}
    return pl.pallas_call(
        functools.partial(terms_kernel, n_terms, start == 0),
        grid_spec=pltpu.PrefetchScalarGridSpec(
            num_scalar_prefetch=1,
            grid=(n_col, steps),
            in_specs=in_specs,
            out_specs=pl.BlockSpec((block, sides), at),
        ),
        out_shape=jax.ShapeDtypeStruct(rhs.shape, F32),
        input_output_aliases=aliases,
        compiler_params=pltpu.CompilerParams(vmem_limit_bytes=VMEM_LIMIT),
        cost_estimate=COST,
        name="terms",
    )(leading, *operands)


def forwarded_call(common, own, column, bufs, weights, start, size, part, combined):
    _, total_weight, rhs, top = common
    width, sides = column.shape[1], rhs.shape[1]
    block = block_rows(size, start, part)
    at = lambda j, s: (s[0] * (part // block) + start // block + j, 0)
    in_specs = [
        pl.BlockSpec(memory_space=pltpu.SMEM),
        pl.BlockSpec((block, sides), at),
        pl.BlockSpec(top.shape, lambda j, s: (0, 0)),
        pl.BlockSpec(weights.shape, lambda j, s: (0, 0)),
        pl.BlockSpec((block, width), at),
    ]
    in_specs += [pl.BlockSpec((block, width), lambda j, s: (j, 0))] * len(bufs)
    operands = [total_weight, rhs, top, weights, column, *bufs]
    aliases = {}
    if combined is not None:
        in_specs.append(ANY)
        operands.append(combined)
        aliases = {len(operands): 0}
    return pl.pallas_call(
        functools.partial(terms_kernel, 1 + len(bufs), False),
        grid_spec=pltpu.PrefetchScalarGridSpec(
            num_scalar_prefetch=1,
            grid=(size // block,),
            in_specs=in_specs,
            out_specs=pl.BlockSpec((block, sides), at),
        ),
        out_shape=jax.ShapeDtypeStruct(rhs.shape, F32),
        input_output_aliases=aliases,
        compiler_params=pltpu.CompilerParams(vmem_limit_bytes=VMEM_LIMIT),
        cost_estimate=COST,
        name="forwarded_terms",
    )(own, *operands)


def split_weights(x):
    high = lax.reduce_precision(x, 8, 7)
    high, low = high.astype(BF16), (x - high).astype(BF16)
    return jnp.concatenate([high, high, low], axis=0)


def body(panel_column, trailing, right_side, term_weights):
    column = panel_column[0]
    rows, width = column.shape
    n_term, n_row, n_col = (lax.axis_size(a) for a in ("term", "row", "col"))
    t, r, c = (lax.axis_index(a) for a in ("term", "row", "col"))
    window = trailing.shape[2]
    sides = right_side.shape[1]
    per_row = window * n_col // n_row
    part = rows // n_col
    sizes = chunk_sizes(part, width)
    starts = [sum(sizes[:i]) for i in range(len(sizes))]
    leading = (r == 0).astype(jnp.int32)[None]
    slots = slot_terms(t, n_term)

    mine = [lax.dynamic_slice_in_dim(column, c * part + o, s, 0) for o, s in zip(starts, sizes)]
    token = jnp.zeros((8, LANES), F32)
    _, bulk = gate(token, [], mine[:2])
    gathered = [lax.all_gather(m, ("term", "col"), axis=0, tiled=True) for m in bulk]

    sent = jnp.concatenate([column[:width], jnp.full((PAD, width), term_weights[0], F32)], axis=0)
    arrived = [(sent,)]
    for h in range(1, n_term):
        arrived.append(merge_hop(h, send_hop(h, arrived[-1], t, n_term), t, n_term))
    _, (held,) = gate(token, [arrived[-1][0]], mine[2:])
    forwarded = [(held,)]
    for h in range(1, n_term - 1):
        forwarded.append(merge_hop(h, send_hop(h, forwarded[-1], t, n_term), t, n_term))

    tops = right_side[:width]
    n_side = sides // LANES
    packed = [column[width : width + per_row]] + [
        tops[:, i * LANES : (i + 1) * LANES] for i in range(n_side)
    ]
    packed = lax.all_gather(jnp.concatenate(packed, axis=0), "row", axis=0)
    window_rows = packed[:, :per_row].reshape(n_row * per_row, width)
    window_rows = lax.dynamic_slice_in_dim(window_rows, c * window, window, 0)
    right_top = jnp.concatenate(
        [packed[0, per_row + i * width : per_row + (i + 1) * width] for i in range(n_side)], axis=1
    )

    heads = [sent]
    for s in range(1, n_term):
        heads.append(
            sum(
                jnp.where((source == s) & valid, arrived[h][place], 0.0)
                for h, place, source, valid in slots
            )
        )
    weights = jnp.stack([h[width, 0] for h in heads])
    total_weight = jnp.sum(weights)[None]
    corner = heads[0][:width]
    for s in range(1, n_term):
        got = lax.ppermute(heads[s][:width], "row", [(0, s)])
        corner = jnp.where(r == s, got, corner)
    lower = jnp.linalg.cholesky(corner)
    inverse = lax.linalg.triangular_solve(
        lower, jnp.eye(width, dtype=F32), left_side=True, lower=True
    )
    inverses = lax.all_gather(inverse, "row", axis=0)[:n_term]

    inverse_t = inverses[0].T
    picked_t = dot(window_rows, inverse_t).T
    factor, updated = factor_call(leading, column, trailing[0], inverse_t, picked_t, lower)

    _, last = gate(token, [factor], list(forwarded[-1]))
    forwarded[-1] = tuple(last)
    h = n_term - 1
    forwarded.append(merge_hop(h, send_hop(h, forwarded[-1], t, n_term), t, n_term))
    forwarded = [forwarded[h][place] for h, place, _, _ in slots]

    solved = [weights[s] * dot(inverses[s], right_top) for s in range(n_term)]
    top = sum(solved)
    tall = jnp.concatenate([dot(inverses[s].T, solved[s]) for s in range(n_term)], axis=0)
    by_term = split_weights(
        lax.dynamic_slice_in_dim(
            jnp.concatenate([tall, tall], axis=0), (n_term - t) * width, n_term * width, 0
        )
    )
    by_hop = [tall[:width]]
    for _, _, source, valid in slots:
        picked = lax.dynamic_slice_in_dim(tall, source * width, width, 0)
        by_hop.append(jnp.where(valid, picked, 0.0))
    by_hop = split_weights(jnp.concatenate(by_hop, axis=0))

    common = (leading, total_weight, right_side, top)
    def of_gather(i, combined, after):
        return terms_call(
            common, gathered[i], by_term, starts[i], sizes[i], n_col, part, combined, after
        )

    combined = of_gather(0, None, [factor])
    _, (passed,) = gate(token, [combined], forwarded[-1:])
    forwarded[-1] = passed
    for k in range(n_col):
        ring = [(i, (i + k) % n_col) for i in range(n_col)]
        bufs = [lax.ppermute(f, "col", ring) for f in forwarded] if k else forwarded
        own = lax.rem(c - k + n_col, n_col).astype(jnp.int32)[None]
        combined = forwarded_call(
            common, own, column, bufs, by_hop, starts[2], sizes[2], part, combined
        )
    combined = of_gather(1, combined, [])
    return (factor[None], updated[None], combined)


def solution(mesh):
    placed = (P("term", "row", None), P("term", "row", "col"), P("row", "col"), P("term"))
    return jax.shard_map(
        body,
        mesh=mesh,
        in_specs=placed,
        out_specs=(P("term", "row", None), P("term", "row", "col"), P("row", "col")),
        check_vma=False,
    )
```

```python
import functools
import math

import jax
import jax.numpy as jnp
from jax import lax
from jax.experimental import pallas as pl
from jax.experimental.pallas import tpu as pltpu
from jax.sharding import PartitionSpec as P

HIGH = lax.Precision.HIGHEST
F32 = jnp.float32
BF16 = jnp.bfloat16
LANES = 128
PAD = 8
VMEM_LIMIT = 60 * 1024 * 1024
ANY = pl.BlockSpec(memory_space=pl.ANY)
COST = pl.CostEstimate(flops=1, bytes_accessed=1, transcendentals=0)


def dot(left, right):
    return jnp.dot(left, right, precision=HIGH, preferred_element_type=F32)


def chunk_sizes(part, width):
    unit = part // 12
    if part % 12 == 0 and unit % width == 0:
        return [8 * unit, unit, 3 * unit]
    return [part - 2 * width, width, width]


def block_rows(*extents, most=512):
    return math.gcd(most, *extents)


def send_hop(h, mine, t, n):
    to_right = [(j, j + 1) for j in range(h - 1, n - 1)]
    to_left = [(j, j - 1) for j in range(1, n - h + 1)]
    if 2 * (h - 1) > n - 1:
        return (lax.ppermute(mine[0], "term", to_right + to_left),)
    return (lax.ppermute(mine[0], "term", to_right), lax.ppermute(mine[-1], "term", to_left))


def merge_hop(h, got, t, n):
    if len(got) == 2 and 2 * h > n - 1:
        return (jnp.where(t >= h, got[0], got[1]),)
    return got


def slot_terms(t, n):
    slots = []
    for h in range(1, n):
        if 2 * h > n - 1:
            slots.append((h, 0, jnp.where(t >= h, n - h, h), (t >= h) | (t < n - h)))
        else:
            slots.append((h, 0, jnp.int32(n - h), t >= h))
            slots.append((h, 1, jnp.int32(h), t < n - h))
    return slots


def gate(token, after, passed):
    def kernel(*refs):
        pass

    first = 1 + len(after)
    outs = [token, *passed]
    got = pl.pallas_call(
        kernel,
        in_specs=[ANY] * (first + len(passed)),
        out_specs=[ANY] * len(outs),
        out_shape=[jax.ShapeDtypeStruct(a.shape, a.dtype) for a in outs],
        input_output_aliases={0: 0} | {first + i: 1 + i for i in range(len(passed))},
        compiler_params=pltpu.CompilerParams(vmem_limit_bytes=VMEM_LIMIT),
        cost_estimate=COST,
        name="gate",
    )(token, *after, *passed)
    return got[0], got[1:]


def factor_kernel(width, flag, panel, trailing, inverse_t, picked_t, lower, factor, updated):
    solved = dot(panel[...], inverse_t[...])
    factor[...] = solved

    @pl.when((pl.program_id(0) == 0) & (flag[0] == 1))
    def _():
        factor[:width] = lower[...]

    updated[...] = trailing[...] - dot(factor[...], picked_t[...])


def factor_call(leading, panel, trailing, inverse_t, picked_t, lower):
    rows, width = panel.shape
    window = trailing.shape[1]
    block = block_rows(rows) * (2 if rows % 1024 == 0 else 1)
    whole = lambda a: pl.BlockSpec(a.shape, lambda i, f: (0, 0))
    tile = lambda n: pl.BlockSpec((block, n), lambda i, f: (i, 0))
    return pl.pallas_call(
        functools.partial(factor_kernel, width),
        grid_spec=pltpu.PrefetchScalarGridSpec(
            num_scalar_prefetch=1,
            grid=(rows // block,),
            in_specs=[tile(width), tile(window), whole(inverse_t), whole(picked_t), whole(lower)],
            out_specs=[tile(width), tile(window)],
        ),
        out_shape=[
            jax.ShapeDtypeStruct((rows, width), F32),
            jax.ShapeDtypeStruct((rows, window), F32),
        ],
        compiler_params=pltpu.CompilerParams(vmem_limit_bytes=VMEM_LIMIT),
        cost_estimate=COST,
        name="factor_update",
    )(leading, panel, trailing, inverse_t, picked_t, lower)


def split(x):
    high = x.astype(BF16)
    return high, (x - high.astype(F32)).astype(BF16)


def terms_kernel(n_terms, first, leading, total_weight, rhs, top, weights, *refs):
    bufs, out = refs[:n_terms], refs[-1]
    high, low = split(jnp.concatenate([b[...] for b in bufs], axis=1))
    stacked = jnp.concatenate([high, low, high], axis=1)
    product = jnp.dot(stacked, weights[...], preferred_element_type=F32)
    out[...] = total_weight[0] * rhs[...] - product
    if first:

        @pl.when((leading[0] == 1) & (pl.program_id(0) == 0) & (pl.program_id(1) == 0))
        def _():
            out[: top.shape[0]] = top[...]


def terms_call(common, gathered, weights, start, size, n_col, part, combined, after):
    leading, total_weight, rhs, top = common
    width, sides = gathered.shape[1], rhs.shape[1]
    n_terms = gathered.shape[0] // (n_col * size)
    block = block_rows(size, start, part, most=1024 if size > 1024 else 512)
    steps = size // block
    at = lambda k, j, s: (k * (part // block) + start // block + j, 0)
    in_specs = [
        pl.BlockSpec(memory_space=pltpu.SMEM),
        pl.BlockSpec((block, sides), at),
        pl.BlockSpec(top.shape, lambda k, j, s: (0, 0)),
        pl.BlockSpec(weights.shape, lambda k, j, s: (0, 0)),
    ]
    in_specs += [
        pl.BlockSpec((block, width), lambda k, j, s, i=i: ((i * n_col + k) * steps + j, 0))
        for i in range(n_terms)
    ]
    operands = [total_weight, rhs, top, weights, *[gathered] * n_terms, *after]
    in_specs += [ANY] * len(after)
    aliases = {}
    if combined is not None:
        in_specs.append(ANY)
        operands.append(combined)
        aliases = {len(operands): 0}
    return pl.pallas_call(
        functools.partial(terms_kernel, n_terms, start == 0),
        grid_spec=pltpu.PrefetchScalarGridSpec(
            num_scalar_prefetch=1,
            grid=(n_col, steps),
            in_specs=in_specs,
            out_specs=pl.BlockSpec((block, sides), at),
        ),
        out_shape=jax.ShapeDtypeStruct(rhs.shape, F32),
        input_output_aliases=aliases,
        compiler_params=pltpu.CompilerParams(vmem_limit_bytes=VMEM_LIMIT),
        cost_estimate=COST,
        name="terms",
    )(leading, *operands)


def forwarded_call(common, own, column, bufs, weights, start, size, part, combined):
    _, total_weight, rhs, top = common
    width, sides = column.shape[1], rhs.shape[1]
    block = block_rows(size, start, part)
    at = lambda j, s: (s[0] * (part // block) + start // block + j, 0)
    in_specs = [
        pl.BlockSpec(memory_space=pltpu.SMEM),
        pl.BlockSpec((block, sides), at),
        pl.BlockSpec(top.shape, lambda j, s: (0, 0)),
        pl.BlockSpec(weights.shape, lambda j, s: (0, 0)),
        pl.BlockSpec((block, width), at),
    ]
    in_specs += [pl.BlockSpec((block, width), lambda j, s: (j, 0))] * len(bufs)
    operands = [total_weight, rhs, top, weights, column, *bufs]
    aliases = {}
    if combined is not None:
        in_specs.append(ANY)
        operands.append(combined)
        aliases = {len(operands): 0}
    return pl.pallas_call(
        functools.partial(terms_kernel, 1 + len(bufs), False),
        grid_spec=pltpu.PrefetchScalarGridSpec(
            num_scalar_prefetch=1,
            grid=(size // block,),
            in_specs=in_specs,
            out_specs=pl.BlockSpec((block, sides), at),
        ),
        out_shape=jax.ShapeDtypeStruct(rhs.shape, F32),
        input_output_aliases=aliases,
        compiler_params=pltpu.CompilerParams(vmem_limit_bytes=VMEM_LIMIT),
        cost_estimate=COST,
        name="forwarded_terms",
    )(own, *operands)


def split_weights(x):
    high = lax.reduce_precision(x, 8, 7)
    high, low = high.astype(BF16), (x - high).astype(BF16)
    return jnp.concatenate([high, high, low], axis=0)


def body(panel_column, trailing, right_side, term_weights):
    column = panel_column[0]
    rows, width = column.shape
    n_term, n_row, n_col = (lax.axis_size(a) for a in ("term", "row", "col"))
    t, r, c = (lax.axis_index(a) for a in ("term", "row", "col"))
    window = trailing.shape[2]
    sides = right_side.shape[1]
    per_row = window * n_col // n_row
    part = rows // n_col
    sizes = chunk_sizes(part, width)
    starts = [sum(sizes[:i]) for i in range(len(sizes))]
    leading = (r == 0).astype(jnp.int32)[None]
    slots = slot_terms(t, n_term)

    mine = [lax.dynamic_slice_in_dim(column, c * part + o, s, 0) for o, s in zip(starts, sizes)]
    token = jnp.zeros((8, LANES), F32)
    _, (bulk,) = gate(token, [], mine[:1])
    gathered = [lax.all_gather(bulk, ("term", "col"), axis=0, tiled=True)]

    sent = jnp.concatenate([column[:width], jnp.full((PAD, width), term_weights[0], F32)], axis=0)
    arrived = [(sent,)]
    for h in range(1, n_term):
        arrived.append(merge_hop(h, send_hop(h, arrived[-1], t, n_term), t, n_term))
    _, (small, held) = gate(token, [arrived[-1][0]], mine[1:])
    gathered.append(lax.all_gather(small, ("term", "col"), axis=0, tiled=True))
    forwarded = [(held,)]
    for h in range(1, n_term - 1):
        forwarded.append(merge_hop(h, send_hop(h, forwarded[-1], t, n_term), t, n_term))

    tops = right_side[:width]
    n_side = sides // LANES
    packed = [column[width : width + per_row]] + [
        tops[:, i * LANES : (i + 1) * LANES] for i in range(n_side)
    ]
    packed = lax.all_gather(jnp.concatenate(packed, axis=0), "row", axis=0)
    window_rows = packed[:, :per_row].reshape(n_row * per_row, width)
    window_rows = lax.dynamic_slice_in_dim(window_rows, c * window, window, 0)
    right_top = jnp.concatenate(
        [packed[0, per_row + i * width : per_row + (i + 1) * width] for i in range(n_side)], axis=1
    )

    heads = [sent]
    for s in range(1, n_term):
        heads.append(
            sum(
                jnp.where((source == s) & valid, arrived[h][place], 0.0)
                for h, place, source, valid in slots
            )
        )
    weights = jnp.stack([h[width, 0] for h in heads])
    total_weight = jnp.sum(weights)[None]
    corner = heads[0][:width]
    for s in range(1, n_term):
        got = lax.ppermute(heads[s][:width], "row", [(0, s)])
        corner = jnp.where(r == s, got, corner)
    lower = jnp.linalg.cholesky(corner)
    inverse = lax.linalg.triangular_solve(
        lower, jnp.eye(width, dtype=F32), left_side=True, lower=True
    )
    inverses = lax.all_gather(inverse, "row", axis=0)[:n_term]

    inverse_t = inverses[0].T
    picked_t = dot(window_rows, inverse_t).T
    factor, updated = factor_call(leading, column, trailing[0], inverse_t, picked_t, lower)

    _, last = gate(token, [factor], list(forwarded[-1]))
    forwarded[-1] = tuple(last)
    h = n_term - 1
    forwarded.append(merge_hop(h, send_hop(h, forwarded[-1], t, n_term), t, n_term))
    forwarded = [forwarded[h][place] for h, place, _, _ in slots]

    solved = [weights[s] * dot(inverses[s], right_top) for s in range(n_term)]
    top = sum(solved)
    tall = jnp.concatenate([dot(inverses[s].T, solved[s]) for s in range(n_term)], axis=0)
    by_term = split_weights(
        lax.dynamic_slice_in_dim(
            jnp.concatenate([tall, tall], axis=0), (n_term - t) * width, n_term * width, 0
        )
    )
    by_hop = [tall[:width]]
    for _, _, source, valid in slots:
        picked = lax.dynamic_slice_in_dim(tall, source * width, width, 0)
        by_hop.append(jnp.where(valid, picked, 0.0))
    by_hop = split_weights(jnp.concatenate(by_hop, axis=0))

    common = (leading, total_weight, right_side, top)
    def of_gather(i, combined, after):
        return terms_call(
            common, gathered[i], by_term, starts[i], sizes[i], n_col, part, combined, after
        )

    combined = of_gather(0, None, [factor])
    _, (passed,) = gate(token, [combined], forwarded[-1:])
    forwarded[-1] = passed
    for k in range(n_col):
        ring = [(i, (i + k) % n_col) for i in range(n_col)]
        bufs = [lax.ppermute(f, "col", ring) for f in forwarded] if k else forwarded
        own = lax.rem(c - k + n_col, n_col).astype(jnp.int32)[None]
        combined = forwarded_call(
            common, own, column, bufs, by_hop, starts[2], sizes[2], part, combined
        )
    combined = of_gather(1, combined, [])
    return (factor[None], updated[None], combined)


def solution(mesh):
    placed = (P("term", "row", None), P("term", "row", "col"), P("row", "col"), P("term"))
    return jax.shard_map(
        body,
        mesh=mesh,
        in_specs=placed,
        out_specs=(P("term", "row", None), P("term", "row", "col"), P("row", "col")),
        check_vma=False,
    )
```

```python
import functools
import math

import jax
import jax.numpy as jnp
from jax import lax
from jax.experimental import pallas as pl
from jax.experimental.pallas import tpu as pltpu
from jax.sharding import PartitionSpec as P

HIGH = lax.Precision.HIGHEST
F32 = jnp.float32
BF16 = jnp.bfloat16
LANES = 128
PAD = 8
VMEM_LIMIT = 60 * 1024 * 1024
ANY = pl.BlockSpec(memory_space=pl.ANY)
COST = pl.CostEstimate(flops=1, bytes_accessed=1, transcendentals=0)


def dot(left, right):
    return jnp.dot(left, right, precision=HIGH, preferred_element_type=F32)


def chunk_sizes(part, width):
    unit = part // 12
    if part % 12 == 0 and unit % width == 0:
        return [8 * unit, unit, 3 * unit]
    return [part - 2 * width, width, width]


def block_rows(*extents, most=512):
    return math.gcd(most, *extents)


def send_hop(h, mine, t, n):
    to_right = [(j, j + 1) for j in range(h - 1, n - 1)]
    to_left = [(j, j - 1) for j in range(1, n - h + 1)]
    if 2 * (h - 1) > n - 1:
        return (lax.ppermute(mine[0], "term", to_right + to_left),)
    return (lax.ppermute(mine[0], "term", to_right), lax.ppermute(mine[-1], "term", to_left))


def merge_hop(h, got, t, n):
    if len(got) == 2 and 2 * h > n - 1:
        return (jnp.where(t >= h, got[0], got[1]),)
    return got


def slot_terms(t, n):
    slots = []
    for h in range(1, n):
        if 2 * h > n - 1:
            slots.append((h, 0, jnp.where(t >= h, n - h, h), (t >= h) | (t < n - h)))
        else:
            slots.append((h, 0, jnp.int32(n - h), t >= h))
            slots.append((h, 1, jnp.int32(h), t < n - h))
    return slots


def gate(token, after, passed):
    def kernel(*refs):
        pass

    first = 1 + len(after)
    outs = [token, *passed]
    got = pl.pallas_call(
        kernel,
        in_specs=[ANY] * (first + len(passed)),
        out_specs=[ANY] * len(outs),
        out_shape=[jax.ShapeDtypeStruct(a.shape, a.dtype) for a in outs],
        input_output_aliases={0: 0} | {first + i: 1 + i for i in range(len(passed))},
        compiler_params=pltpu.CompilerParams(vmem_limit_bytes=VMEM_LIMIT),
        cost_estimate=COST,
        name="gate",
    )(token, *after, *passed)
    return got[0], got[1:]


def factor_kernel(width, flag, panel, trailing, inverse_t, picked_t, lower, factor, updated):
    both = dot(panel[...], jnp.concatenate([inverse_t[...], picked_t[...]], axis=1))
    factor[...] = both[:, :width]
    updated[...] = trailing[...] - both[:, width:]

    @pl.when((pl.program_id(0) == 0) & (flag[0] == 1))
    def _():
        factor[:width] = lower[...]


def factor_call(leading, panel, trailing, inverse_t, picked_t, lower):
    rows, width = panel.shape
    window = trailing.shape[1]
    block = block_rows(rows) * (2 if rows % 1024 == 0 else 1)
    whole = lambda a: pl.BlockSpec(a.shape, lambda i, f: (0, 0))
    tile = lambda n: pl.BlockSpec((block, n), lambda i, f: (i, 0))
    return pl.pallas_call(
        functools.partial(factor_kernel, width),
        grid_spec=pltpu.PrefetchScalarGridSpec(
            num_scalar_prefetch=1,
            grid=(rows // block,),
            in_specs=[tile(width), tile(window), whole(inverse_t), whole(picked_t), whole(lower)],
            out_specs=[tile(width), tile(window)],
        ),
        out_shape=[
            jax.ShapeDtypeStruct((rows, width), F32),
            jax.ShapeDtypeStruct((rows, window), F32),
        ],
        compiler_params=pltpu.CompilerParams(vmem_limit_bytes=VMEM_LIMIT),
        cost_estimate=COST,
        name="factor_update",
    )(leading, panel, trailing, inverse_t, picked_t, lower)


def split(x):
    high = x.astype(BF16)
    return high, (x - high.astype(F32)).astype(BF16)


def terms_kernel(n_terms, first, leading, total_weight, rhs, top, weights, *refs):
    bufs, out = refs[:n_terms], refs[-1]
    high, low = split(jnp.concatenate([b[...] for b in bufs], axis=1))
    stacked = jnp.concatenate([high, low, high], axis=1)
    product = jnp.dot(stacked, weights[...], preferred_element_type=F32)
    out[...] = total_weight[0] * rhs[...] - product
    if first:

        @pl.when((leading[0] == 1) & (pl.program_id(0) == 0) & (pl.program_id(1) == 0))
        def _():
            out[: top.shape[0]] = top[...]


def terms_call(common, gathered, weights, start, size, n_col, part, combined, after):
    leading, total_weight, rhs, top = common
    width, sides = gathered.shape[1], rhs.shape[1]
    n_terms = gathered.shape[0] // (n_col * size)
    block = block_rows(size, start, part, most=1024 if size > 1024 else 512)
    steps = size // block
    at = lambda k, j, s: (k * (part // block) + start // block + j, 0)
    in_specs = [
        pl.BlockSpec(memory_space=pltpu.SMEM),
        pl.BlockSpec((block, sides), at),
        pl.BlockSpec(top.shape, lambda k, j, s: (0, 0)),
        pl.BlockSpec(weights.shape, lambda k, j, s: (0, 0)),
    ]
    in_specs += [
        pl.BlockSpec((block, width), lambda k, j, s, i=i: ((i * n_col + k) * steps + j, 0))
        for i in range(n_terms)
    ]
    operands = [total_weight, rhs, top, weights, *[gathered] * n_terms, *after]
    in_specs += [ANY] * len(after)
    aliases = {}
    if combined is not None:
        in_specs.append(ANY)
        operands.append(combined)
        aliases = {len(operands): 0}
    return pl.pallas_call(
        functools.partial(terms_kernel, n_terms, start == 0),
        grid_spec=pltpu.PrefetchScalarGridSpec(
            num_scalar_prefetch=1,
            grid=(n_col, steps),
            in_specs=in_specs,
            out_specs=pl.BlockSpec((block, sides), at),
        ),
        out_shape=jax.ShapeDtypeStruct(rhs.shape, F32),
        input_output_aliases=aliases,
        compiler_params=pltpu.CompilerParams(vmem_limit_bytes=VMEM_LIMIT),
        cost_estimate=COST,
        name="terms",
    )(leading, *operands)


def forwarded_call(common, own, column, bufs, weights, start, size, part, combined):
    _, total_weight, rhs, top = common
    width, sides = column.shape[1], rhs.shape[1]
    block = block_rows(size, start, part)
    at = lambda j, s: (s[0] * (part // block) + start // block + j, 0)
    in_specs = [
        pl.BlockSpec(memory_space=pltpu.SMEM),
        pl.BlockSpec((block, sides), at),
        pl.BlockSpec(top.shape, lambda j, s: (0, 0)),
        pl.BlockSpec(weights.shape, lambda j, s: (0, 0)),
        pl.BlockSpec((block, width), at),
    ]
    in_specs += [pl.BlockSpec((block, width), lambda j, s: (j, 0))] * len(bufs)
    operands = [total_weight, rhs, top, weights, column, *bufs]
    aliases = {}
    if combined is not None:
        in_specs.append(ANY)
        operands.append(combined)
        aliases = {len(operands): 0}
    return pl.pallas_call(
        functools.partial(terms_kernel, 1 + len(bufs), False),
        grid_spec=pltpu.PrefetchScalarGridSpec(
            num_scalar_prefetch=1,
            grid=(size // block,),
            in_specs=in_specs,
            out_specs=pl.BlockSpec((block, sides), at),
        ),
        out_shape=jax.ShapeDtypeStruct(rhs.shape, F32),
        input_output_aliases=aliases,
        compiler_params=pltpu.CompilerParams(vmem_limit_bytes=VMEM_LIMIT),
        cost_estimate=COST,
        name="forwarded_terms",
    )(own, *operands)


def split_weights(x):
    high = lax.reduce_precision(x, 8, 7)
    high, low = high.astype(BF16), (x - high).astype(BF16)
    return jnp.concatenate([high, high, low], axis=0)


def body(panel_column, trailing, right_side, term_weights):
    column = panel_column[0]
    rows, width = column.shape
    n_term, n_row, n_col = (lax.axis_size(a) for a in ("term", "row", "col"))
    t, r, c = (lax.axis_index(a) for a in ("term", "row", "col"))
    window = trailing.shape[2]
    sides = right_side.shape[1]
    per_row = window * n_col // n_row
    part = rows // n_col
    sizes = chunk_sizes(part, width)
    starts = [sum(sizes[:i]) for i in range(len(sizes))]
    leading = (r == 0).astype(jnp.int32)[None]
    slots = slot_terms(t, n_term)

    mine = [lax.dynamic_slice_in_dim(column, c * part + o, s, 0) for o, s in zip(starts, sizes)]
    token = jnp.zeros((8, LANES), F32)
    _, (bulk,) = gate(token, [], mine[:1])
    gathered = [lax.all_gather(bulk, ("term", "col"), axis=0, tiled=True)]

    sent = jnp.concatenate([column[:width], jnp.full((PAD, width), term_weights[0], F32)], axis=0)
    arrived = [(sent,)]
    for h in range(1, n_term):
        arrived.append(merge_hop(h, send_hop(h, arrived[-1], t, n_term), t, n_term))
    _, (small, held) = gate(token, [arrived[-1][0]], mine[1:])
    gathered.append(lax.all_gather(small, ("term", "col"), axis=0, tiled=True))
    forwarded = [(held,)]
    for h in range(1, n_term - 1):
        forwarded.append(merge_hop(h, send_hop(h, forwarded[-1], t, n_term), t, n_term))

    tops = right_side[:width]
    n_side = sides // LANES
    packed = [column[width : width + per_row]] + [
        tops[:, i * LANES : (i + 1) * LANES] for i in range(n_side)
    ]
    packed = lax.all_gather(jnp.concatenate(packed, axis=0), "row", axis=0)
    window_rows = packed[:, :per_row].reshape(n_row * per_row, width)
    window_rows = lax.dynamic_slice_in_dim(window_rows, c * window, window, 0)
    right_top = jnp.concatenate(
        [packed[0, per_row + i * width : per_row + (i + 1) * width] for i in range(n_side)], axis=1
    )

    heads = [sent]
    for s in range(1, n_term):
        heads.append(
            sum(
                jnp.where((source == s) & valid, arrived[h][place], 0.0)
                for h, place, source, valid in slots
            )
        )
    weights = jnp.stack([h[width, 0] for h in heads])
    total_weight = jnp.sum(weights)[None]
    corner = heads[0][:width]
    for s in range(1, n_term):
        got = lax.ppermute(heads[s][:width], "row", [(0, s)])
        corner = jnp.where(r == s, got, corner)
    lower = jnp.linalg.cholesky(corner)
    inverse = lax.linalg.triangular_solve(
        lower, jnp.eye(width, dtype=F32), left_side=True, lower=True
    )
    inverses = lax.all_gather(inverse, "row", axis=0)[:n_term]

    inverse_t = inverses[0].T
    picked_t = dot(inverse_t, dot(window_rows, inverse_t).T)
    factor, updated = factor_call(leading, column, trailing[0], inverse_t, picked_t, lower)

    _, last = gate(token, [factor], list(forwarded[-1]))
    forwarded[-1] = tuple(last)
    h = n_term - 1
    forwarded.append(merge_hop(h, send_hop(h, forwarded[-1], t, n_term), t, n_term))
    forwarded = [forwarded[h][place] for h, place, _, _ in slots]

    solved = [weights[s] * dot(inverses[s], right_top) for s in range(n_term)]
    top = sum(solved)
    tall = jnp.concatenate([dot(inverses[s].T, solved[s]) for s in range(n_term)], axis=0)
    by_term = split_weights(
        lax.dynamic_slice_in_dim(
            jnp.concatenate([tall, tall], axis=0), (n_term - t) * width, n_term * width, 0
        )
    )
    by_hop = [tall[:width]]
    for _, _, source, valid in slots:
        picked = lax.dynamic_slice_in_dim(tall, source * width, width, 0)
        by_hop.append(jnp.where(valid, picked, 0.0))
    by_hop = split_weights(jnp.concatenate(by_hop, axis=0))

    common = (leading, total_weight, right_side, top)
    def of_gather(i, combined, after):
        return terms_call(
            common, gathered[i], by_term, starts[i], sizes[i], n_col, part, combined, after
        )

    combined = of_gather(0, None, [factor])
    _, (passed,) = gate(token, [combined], forwarded[-1:])
    forwarded[-1] = passed
    for k in range(n_col):
        ring = [(i, (i + k) % n_col) for i in range(n_col)]
        bufs = [lax.ppermute(f, "col", ring) for f in forwarded] if k else forwarded
        own = lax.rem(c - k + n_col, n_col).astype(jnp.int32)[None]
        combined = forwarded_call(
            common, own, column, bufs, by_hop, starts[2], sizes[2], part, combined
        )
    combined = of_gather(1, combined, [])
    return (factor[None], updated[None], combined)


def solution(mesh):
    placed = (P("term", "row", None), P("term", "row", "col"), P("row", "col"), P("term"))
    return jax.shard_map(
        body,
        mesh=mesh,
        in_specs=placed,
        out_specs=(P("term", "row", None), P("term", "row", "col"), P("row", "col")),
        check_vma=False,
    )
```
